32 devices in a mesh: cell: 8 (over z, y), tm: 4 (over x, core).
Axes of the slice: x: 2, y: 2, z: 4, core: 2. Of those that a mesh axis runs over, the one named last changes fastest.
Arguments:
- snapshots: float32 [384, 5, 6144], P('tm', None, 'cell'), may hold values from -6 to 6
- volumes: float32 [6144], P('cell'), may hold values from 0.1 to 10
- freq_index: int32 [8], replicated, may hold values from 1 to 63, as said below
- block_start: int32 [5], replicated, may hold values from 0 to 256, as said below
Outputs:
- modes: float32 [8, 10, 5, 6144], P('tm', None, None, 'cell')
- triangle: float32 [8, 10, 10], P('tm')
The draws below stay inside these ranges and needn't reach their ends.
Inputs may be any that keep to these rules, and one draw needn't show every extreme that they name: `freq_index`: distinct indices; the smallest and the largest allowed value both occur. `block_start`: rising; the first is 0 and the last is 256; with s = 64, start b lies within s // 4 of b * s.
All inputs are finite; a program needn't handle non-finite values.
Results may differ from the reference program's by a relative error of at most 0.000078.
Values sent between devices are 32-bit elements; how exact they have to be, the bound alone decides.
A program may use at most 64 MiB of HBM per device.

```python
import math
import jax
import jax.numpy as jnp
from jax import lax

V = 5
NFFT = 128
NF = 8
NB = 5
TSNAP = 384
NCELL = 6144


def draw_freq_index(key, part):
    picked = jax.random.permutation(key, NFFT // 2 - 3)[:NF - 2].astype(jnp.int32) + 2
    return jnp.concatenate([jnp.array([1], jnp.int32), picked, jnp.array([NFFT // 2 - 1], jnp.int32)])


def draw_block_start(key, part):
    step_size = (TSNAP - NFFT) // (NB - 1)
    jitter_most = step_size // 4
    jitter = jax.random.randint(key, (NB - 2,), -jitter_most, jitter_most + 1).astype(jnp.int32)
    middle = (jnp.arange(1, NB - 1, dtype=jnp.int32) * step_size + jitter).astype(jnp.int32)
    return jnp.concatenate([jnp.array([0], jnp.int32), middle, jnp.array([TSNAP - NFFT], jnp.int32)])


def block_levels(stream_key, shape, shards, least, largest):
    def one(position, parts):
        steps = jax.random.uniform(jax.random.fold_in(jax.random.fold_in(stream_key, 6), position), (parts,), jnp.float32, least / len(shards), largest / len(shards))
        return jnp.repeat(jnp.exp(steps), shape[position] // parts).reshape((-1,) + (1,) * (len(shape) - position - 1))

    factor_of = one(*shards[0])
    for cut in shards[1:]:
        factor_of = factor_of * one(*cut)
    return factor_of


def normal_values(rng, shape, deviation, bound, shards=(), held_as=jnp.bfloat16):
    drawn = deviation * jax.random.normal(rng, shape, jnp.float32)
    if shards:
        drawn = drawn * block_levels(rng, shape, shards, -0.22, 0.18)
    return jnp.clip(drawn, -bound, bound).astype(held_as)


def setup_inputs(seed: int = 0) -> dict:
    key_list = jax.random.split(jax.random.key(seed), 5)
    snapshots = normal_values(key_list[0], (TSNAP, V, NCELL), 1.0, 6.0, ((0, 4), (2, 8)), jnp.float32)
    volumes = jnp.clip(jnp.exp(math.log(10.0) - 4.6051702 * jax.random.uniform(key_list[1], (NCELL,), jnp.float32) ** block_levels(key_list[1], (NCELL,), ((0, 8),), -0.2, 0.2)), 0.1, 10.0)
    freq_index = draw_freq_index(jax.random.fold_in(key_list[4], 71), 0)
    block_start = draw_block_start(jax.random.fold_in(key_list[4], 71), 0)
    return {"snapshots": snapshots, "volumes": volumes, "freq_index": freq_index, "block_start": block_start}


def make_table(freq_index, block_start, times):
    tau = times[None, :] - block_start[:, None]
    valid = (tau >= 0) & (tau < NFFT)
    tauf = tau.astype(jnp.float32)
    hann = jnp.where(valid, 0.5 - 0.5 * jnp.cos(2.0 * jnp.pi * tauf / NFFT), 0.0)
    phase = jnp.mod(freq_index[:, None, None] * tau[None, :, :], NFFT).astype(jnp.float32)
    angle = 2.0 * jnp.pi * phase / NFFT
    real_part = hann[None] * jnp.cos(angle)
    imag_part = -hann[None] * jnp.sin(angle)
    table = jnp.stack([real_part, imag_part], axis=1)
    return table.reshape(NF * 2 * NB, times.shape[0]).astype(jnp.float32)

def reference(snapshots, volumes, freq_index, block_start):
    times = jnp.arange(TSNAP, dtype=jnp.int32)
    table = make_table(freq_index, block_start, times)
    flat = snapshots.reshape(TSNAP, V * NCELL)
    spectra = jnp.dot(table.astype(jnp.float32), flat.astype(jnp.float32), precision=lax.Precision.HIGHEST, preferred_element_type=jnp.float32)
    spectra = spectra.reshape(NF, 2 * NB, V, NCELL)
    weighted = spectra * jnp.sqrt(volumes)[None, None, None, :]
    weighted = weighted.reshape(NF, 2 * NB, V * NCELL)
    gram = jnp.einsum('frc,fsc->frs', weighted, weighted, precision=lax.Precision.HIGHEST)
    lower = jnp.linalg.cholesky(gram)
    solved = jax.vmap(lambda a, b: jax.scipy.linalg.solve_triangular(a, b, lower=True))(lower, weighted)
    modes = (jnp.sqrt(jnp.float32(V * NCELL)) * solved).reshape(NF, 2 * NB, V, NCELL)
    triangle = jnp.transpose(lower, (0, 2, 1)) / jnp.sqrt(jnp.float32(V * NCELL * NFFT))
    return (modes, triangle)
```

```python
import functools

import jax
import jax.numpy as jnp
from jax import lax
from jax.experimental import pallas as pl
from jax.experimental.pallas import tpu as pltpu
from jax.sharding import PartitionSpec as P

NFFT = 128
MESH = pl.DeviceIdType.MESH
F32 = jnp.float32
BF16 = jnp.bfloat16
NT = (((1,), (1,)), ((), ()))
ROWS = 32


def split3(a):
    high = a.astype(BF16)
    rest = a - high.astype(F32)
    middle = rest.astype(BF16)
    low = (rest - middle.astype(F32)).astype(BF16)
    return high, middle, low


def exact_dot(a, b, dims=(((1,), (0,)), ((), ()))):
    return lax.dot_general(
        a, b, dims, precision=lax.Precision.HIGHEST, preferred_element_type=F32
    )


def kernel(
    sizes,
    x_ref,
    vol_ref,
    freq_ref,
    start_ref,
    modes_ref,
    tri_ref,
    snap,
    part,
    got,
    wcat,
    grams,
    local_sem,
    xsend_sem,
    xrecv_sem,
    psend_sem,
    precv_sem,
    gsend_sem,
    grecv_sem,
):
    cell_count, tdev, nvar, cells, nf, nb = sizes
    fdev = nf // 4
    kept = nb - 1
    half = cells // 2
    span = 2 * tdev
    per = kept * 2 * fdev
    rows = nf * 2 * kept
    cell = lax.axis_index("cell")
    tm = lax.axis_index("tm")
    group, core = tm // 2, lax.rem(tm, 2)
    partner = group * 2 + 1 - core
    targets = ((1 - group) * 2 + core, (1 - group) * 2 + 1 - core, partner)

    my_rows = pl.ds(pl.multiple_of(core * tdev, 8), tdev)
    my_cells = pl.ds(pl.multiple_of(core * half, 128), half)
    other_cells = pl.ds(pl.multiple_of((1 - core) * half, 128), half)

    local = []
    for v in range(nvar):
        copy = pltpu.make_async_copy(
            x_ref.at[v, :, my_cells], snap.at[v, my_rows, :], local_sem.at[v]
        )
        copy.start()
        local.append(copy)

    barrier = pltpu.get_barrier_semaphore()
    for target in targets:
        pl.semaphore_signal(barrier, inc=1, device_id={"tm": target}, device_id_type=MESH)
    for step in range(1, cell_count):
        pl.semaphore_signal(
            barrier,
            inc=1,
            device_id={"cell": lax.rem(cell + step, cell_count)},
            device_id_type=MESH,
        )

    row = lax.broadcasted_iota(jnp.int32, (rows, span), 0)
    time = lax.broadcasted_iota(jnp.int32, (rows, span), 1) + group * span
    imag = row % 2
    row_block = (row // (2 * fdev)) % kept
    row_freq = (row // per) * fdev + (row // 2) % fdev
    start = jnp.zeros((rows, span), jnp.int32)
    for b in range(kept):
        start = jnp.where(row_block == b, start_ref[group + b], start)
    freq = jnp.zeros((rows, span), jnp.int32)
    for f in range(nf):
        freq = jnp.where(row_freq == f, freq_ref[f], freq)
    tau = time - start
    valid = (tau >= 0) & (tau < NFFT)
    turn = 2.0 * jnp.pi / NFFT
    hann = jnp.where(valid, 0.5 - 0.5 * jnp.cos((tau & (NFFT - 1)).astype(F32) * turn), 0.0)

    pl.semaphore_wait(barrier, len(targets) + cell_count - 1)

    exchange = []
    for v in range(nvar):
        copy = pltpu.make_async_remote_copy(
            src_ref=x_ref.at[v, :, other_cells],
            dst_ref=snap.at[v, my_rows, :],
            send_sem=xsend_sem.at[v],
            recv_sem=xrecv_sem.at[v],
            device_id={"tm": partner},
            device_id_type=MESH,
        )
        copy.start()
        exchange.append(copy)

    phase = (freq * tau + imag * (NFFT // 4)) & (NFFT - 1)
    table = hann * jnp.cos(phase.astype(F32) * turn)
    th, tmid, tl = split3(table)
    table3 = jnp.concatenate([th, tmid, tl], axis=0)

    sends = []
    for v in range(nvar):
        local[v].wait()
        exchange[v].wait_recv()
        sh, sm, sl = split3(snap[v])
        a = jnp.dot(table3, sh, preferred_element_type=F32)
        b = jnp.dot(table3[: 2 * rows], sm, preferred_element_type=F32)
        c = jnp.dot(th, sl, preferred_element_type=F32)
        small = a[2 * rows :] + b[rows:] + c
        part[v] = a[:rows] + ((a[rows : 2 * rows] + b[:rows]) + small)
        for k, target in enumerate(targets):
            copy = pltpu.make_async_remote_copy(
                src_ref=part.at[v, pl.ds(pl.multiple_of(target * per, 8), per), :],
                dst_ref=got.at[group, v, :, my_cells],
                send_sem=psend_sem.at[k, v],
                recv_sem=precv_sem.at[k, v],
                device_id={"tm": target},
                device_id_type=MESH,
            )
            copy.start()
            sends.append((v, copy))
        got[group, v, :, my_cells] = part[v, pl.ds(pl.multiple_of(tm * per, 8), per), :]

    root = jnp.sqrt(vol_ref[...])
    gram = jnp.zeros((3 * ROWS, 128), F32)
    for v in range(nvar):
        for w, copy in sends:
            if w == v:
                copy.wait_recv()
        pad = jnp.zeros((ROWS - per, cells), F32)
        first = jnp.concatenate([got[0, v], pad], axis=0)
        second = pltpu.roll(jnp.concatenate([got[1, v], pad], axis=0), 2 * fdev, 0)
        weighted = (first + second) * root
        wh, wm, wl = split3(weighted)
        wcat[v] = jnp.concatenate([wh, wm, wl, wh, wm, wh], axis=0)
        lhs = jnp.concatenate([wh, wm, wl], axis=0)
        rhs = jnp.concatenate([wh, wm, wl, jnp.zeros_like(wh)], axis=0)
        gram = gram + lax.dot_general(lhs, rhs, NT, preferred_element_type=F32)

    lane = lax.broadcasted_iota(jnp.int32, (ROWS, 128), 1)
    line = lax.broadcasted_iota(jnp.int32, (ROWS, 128), 0)
    gram = gram[:ROWS] + (gram[ROWS : 2 * ROWS] + gram[2 * ROWS :])
    gram = gram + (pltpu.roll(gram, 128 - ROWS, 1) + pltpu.roll(gram, 128 - 2 * ROWS, 1))
    gram = jnp.where(lane < ROWS, gram, 0.0)
    packed = gram[0:8]
    for q in range(1, ROWS // 8):
        packed = packed + pltpu.roll(gram[8 * q : 8 * q + 8], ROWS * q, 1)
    grams[cell] = packed

    gsends = []
    for step in range(1, cell_count):
        copy = pltpu.make_async_remote_copy(
            src_ref=grams.at[cell],
            dst_ref=grams.at[cell],
            send_sem=gsend_sem.at[step],
            recv_sem=grecv_sem.at[step],
            device_id={"cell": lax.rem(cell + step, cell_count)},
            device_id_type=MESH,
        )
        copy.start()
        gsends.append(copy)
    for copy in gsends:
        copy.wait_recv()
    total = grams[0]
    for q in range(1, cell_count):
        total = total + grams[q]

    pieces = [total] + [pltpu.roll(total, 128 - ROWS * q, 1) for q in range(1, ROWS // 8)]
    full = jnp.concatenate(pieces, axis=0)
    aug = jnp.where(lane < ROWS, full, jnp.where(lane - ROWS == line, 1.0, 0.0))
    columns = 2 * nb
    used = fdev * columns
    line_freq = (line // 2) % fdev
    order = jnp.where(line < used, (line % 2) * nb + line // (2 * fdev), -1)
    for j in range(columns - 1):
        base = (j % nb) * 2 * fdev + j // nb
        pivot = aug[base : base + 1, :]
        where = jnp.full((ROWS, 128), base, jnp.int32)
        for f in range(1, fdev):
            pivot = jnp.where(line_freq == f, aug[base + 2 * f : base + 2 * f + 1, :], pivot)
            where = jnp.where(line_freq == f, base + 2 * f, where)
        hit = lane == where
        column = jnp.sum(jnp.where(hit, aug, 0.0), axis=1, keepdims=True)
        diagonal = jnp.sum(jnp.where(hit, pivot, 0.0), axis=1, keepdims=True)
        factor = jnp.where(order > j, column / diagonal, 0.0)
        aug = aug - factor * pivot
    diagonal = jnp.sum(jnp.where(lane == line, aug, 0.0), axis=1, keepdims=True)
    diagonal = jnp.where(line < used, diagonal, 1.0)
    aug = aug * (1.0 / jnp.sqrt(diagonal))

    total_rows = nvar * cells * cell_count
    out_row = lax.broadcasted_iota(jnp.int32, (ROWS, ROWS), 0)
    in_row = lax.broadcasted_iota(jnp.int32, (ROWS, ROWS), 1)
    place = ((in_row % 2) * nb + in_row // (2 * fdev)) * fdev + (in_row // 2) % fdev
    permute = jnp.where((in_row < used) & (out_row == place), 1.0, 0.0)
    solve = exact_dot(permute, aug) * jnp.sqrt(F32(total_rows))
    solve = jnp.where((lane >= ROWS) & (lane < 2 * ROWS), solve, 0.0)
    solve = solve + pltpu.roll(solve, 2 * ROWS, 1)
    solve = solve + pltpu.roll(solve, ROWS, 1)
    eh, em, el = [e.astype(F32) for e in split3(solve)]
    lhs = jnp.concatenate(
        [
            jnp.where(lane < 3 * ROWS, eh, em),
            jnp.where(lane < ROWS, em, jnp.where(lane < 2 * ROWS, el, 0.0)),
        ],
        axis=1,
    )[:, : 6 * ROWS].astype(BF16)
    for v in range(nvar):
        modes = jnp.dot(lhs, wcat[v], preferred_element_type=F32)
        for j in range(columns):
            modes_ref[j, v, :, :] = modes[j * fdev : (j + 1) * fdev, :]

    tri_row = lax.broadcasted_iota(jnp.int32, (16, ROWS), 0)
    tri_in = lax.broadcasted_iota(jnp.int32, (16, ROWS), 1)
    tri_out = lax.broadcasted_iota(jnp.int32, (16, 128), 0)
    tri_lane = lax.broadcasted_iota(jnp.int32, (16, 128), 1)

    def picks(out, inner, f):
        match = ((inner % 2) * nb + inner // (2 * fdev) == out) & ((inner // 2) % fdev == f)
        return jnp.where(match & (inner < used), 1.0, 0.0)

    tri_scale = F32(1.0) / jnp.sqrt(F32(total_rows * NFFT))
    upper = lax.broadcasted_iota(jnp.int32, (16, 16), 0) <= lax.broadcasted_iota(
        jnp.int32, (16, 16), 1
    )
    for f in range(fdev):
        left = exact_dot(picks(tri_row, tri_in, f), aug)
        both = exact_dot(left, picks(tri_out, tri_lane, f), NT)
        tri = jnp.where(upper, both * tri_scale, 0.0)
        tri_ref[f] = tri[:columns, :columns]

    for copy in exchange:
        copy.wait_send()
    for _, copy in sends:
        copy.wait_send()
    for copy in gsends:
        copy.wait_send()


def on_device(snapshots, volumes, freq_index, block_start):
    tdev, nvar, cells = snapshots.shape
    cell_count = lax.axis_size("cell")
    nf, nb = freq_index.shape[0], block_start.shape[0]
    fdev = nf // lax.axis_size("tm")
    columns = 2 * nb
    kept = nb - 1
    half = cells // 2
    per = kept * 2 * fdev
    sizes = (cell_count, tdev, nvar, cells, nf, nb)
    dma = pltpu.SemaphoreType.DMA
    modes, triangle = pl.pallas_call(
        functools.partial(kernel, sizes),
        out_shape=(
            jax.ShapeDtypeStruct((columns, nvar, fdev, cells), F32),
            jax.ShapeDtypeStruct((fdev, columns, columns), F32),
        ),
        in_specs=[
            pl.BlockSpec(memory_space=pl.ANY),
            pl.BlockSpec(memory_space=pltpu.VMEM),
            pl.BlockSpec(memory_space=pltpu.SMEM),
            pl.BlockSpec(memory_space=pltpu.SMEM),
        ],
        out_specs=(
            pl.BlockSpec(memory_space=pltpu.VMEM),
            pl.BlockSpec(memory_space=pltpu.VMEM),
        ),
        scratch_shapes=[
            pltpu.VMEM((nvar, 2 * tdev, half), F32),
            pltpu.VMEM((nvar, nf * 2 * kept, half), F32),
            pltpu.VMEM((2, nvar, per, cells), F32),
            pltpu.VMEM((nvar, 6 * ROWS, cells), BF16),
            pltpu.VMEM((cell_count, 8, 128), F32),
            dma((nvar,)),
            dma((nvar,)),
            dma((nvar,)),
            dma((3, nvar)),
            dma((3, nvar)),
            dma((cell_count,)),
            dma((cell_count,)),
        ],
        compiler_params=pltpu.CompilerParams(
            collective_id=0, has_side_effects=True, vmem_limit_bytes=32 * 1024 * 1024
        ),
    )(jnp.transpose(snapshots, (1, 0, 2)), volumes.reshape(1, cells), freq_index, block_start)
    return jnp.transpose(modes, (2, 0, 1, 3)), triangle


def solution(mesh):
    placed = (P("tm", None, "cell"), P("cell"), P(), P())
    return jax.shard_map(
        on_device,
        mesh=mesh,
        in_specs=placed,
        out_specs=(P("tm", None, None, "cell"), P("tm", None, None)),
        check_vma=False,
    )
```

```python
import functools
import math

import jax
import jax.numpy as jnp
from jax import lax
from jax.experimental import pallas as pl
from jax.experimental.pallas import tpu as pltpu
from jax.sharding import PartitionSpec as P

NFFT = 128
MESH = pl.DeviceIdType.MESH
F32 = jnp.float32
BF16 = jnp.bfloat16
NT = (((1,), (1,)), ((), ()))
ROWS = 32


def split3(a):
    high = a.astype(BF16)
    rest = a - high.astype(F32)
    middle = rest.astype(BF16)
    low = (rest - middle.astype(F32)).astype(BF16)
    return high, middle, low


def exact_dot(a, b, dims=(((1,), (0,)), ((), ()))):
    return lax.dot_general(
        a, b, dims, precision=lax.Precision.HIGHEST, preferred_element_type=F32
    )


def half_sine_squared(step):
    near = ((step + NFFT // 2) & (NFFT - 1)) - NFFT // 2
    u = near.astype(F32) * (math.pi / NFFT)
    square = u * u
    total = jnp.full_like(u, 1.0 / math.factorial(13))
    for power in (11, 9, 7, 5, 3, 1):
        sign = 1.0 if power % 4 == 1 else -1.0
        total = total * square + sign / math.factorial(power)
    sine = u * total
    return sine * sine


def gather_kernel(
    sizes,
    x_ref,
    vol_hbm,
    freq_hbm,
    start_hbm,
    wcat_hbm,
    total_hbm,
    wcat,
    total_ref,
    snap,
    part,
    got,
    grams,
    vol_ref,
    freq_ref,
    start_ref,
    small_sem,
    local_sem,
    xsend_sem,
    xrecv_sem,
    psend_sem,
    precv_sem,
    gsend_sem,
    grecv_sem,
    out_sem,
):
    cell_count, tdev, nvar, cells, nf, nb = sizes
    fdev = nf // 4
    kept = nb - 1
    half = cells // 2
    span = 2 * tdev
    per = kept * 2 * fdev
    rows = nf * 2 * kept
    cell = lax.axis_index("cell")
    tm = lax.axis_index("tm")
    group, core = tm // 2, lax.rem(tm, 2)
    partner = group * 2 + 1 - core
    targets = ((1 - group) * 2 + core, (1 - group) * 2 + 1 - core, partner)

    my_rows = pl.ds(pl.multiple_of(core * tdev, 8), tdev)
    my_cells = pl.ds(pl.multiple_of(core * half, 128), half)
    other_cells = pl.ds(pl.multiple_of((1 - core) * half, 128), half)

    small = []
    for k, (src, dst) in enumerate(
        ((freq_hbm, freq_ref), (start_hbm, start_ref), (vol_hbm, vol_ref))
    ):
        copy = pltpu.make_async_copy(src, dst, small_sem.at[k])
        copy.start()
        small.append(copy)
    local = []
    for v in range(nvar):
        copy = pltpu.make_async_copy(
            x_ref.at[v, :, my_cells], snap.at[v, my_rows, :], local_sem.at[v]
        )
        copy.start()
        local.append(copy)

    barrier = pltpu.get_barrier_semaphore()
    for target in targets:
        pl.semaphore_signal(barrier, inc=1, device_id={"tm": target}, device_id_type=MESH)
    for step in range(1, cell_count):
        pl.semaphore_signal(
            barrier,
            inc=1,
            device_id={"cell": lax.rem(cell + step, cell_count)},
            device_id_type=MESH,
        )

    pl.semaphore_wait(barrier, len(targets) + cell_count - 1)

    exchange = []
    for v in range(nvar):
        copy = pltpu.make_async_remote_copy(
            src_ref=x_ref.at[v, :, other_cells],
            dst_ref=snap.at[v, my_rows, :],
            send_sem=xsend_sem.at[v],
            recv_sem=xrecv_sem.at[v],
            device_id={"tm": partner},
            device_id_type=MESH,
        )
        copy.start()
        exchange.append(copy)

    for copy in small:
        copy.wait()
    row = lax.broadcasted_iota(jnp.int32, (rows, span), 0)
    time = lax.broadcasted_iota(jnp.int32, (rows, span), 1) + group * span
    imag = row % 2
    row_block = (row // (2 * fdev)) % kept
    row_freq = (row // per) * fdev + (row // 2) % fdev
    start = jnp.zeros((rows, span), jnp.int32)
    for b in range(kept):
        start = jnp.where(row_block == b, start_ref[group + b], start)
    freq = jnp.zeros((rows, span), jnp.int32)
    for f in range(nf):
        freq = jnp.where(row_freq == f, freq_ref[f], freq)
    tau = time - start
    valid = (tau >= 0) & (tau < NFFT)
    hann = jnp.where(valid, half_sine_squared(tau), 0.0)
    table = hann * (1.0 - 2.0 * half_sine_squared(freq * tau + imag * (NFFT // 4)))
    th, tmid, tl = split3(table)
    table3 = jnp.concatenate([th, tmid, tl], axis=0)

    sends = []
    for v in range(nvar):
        local[v].wait()
        exchange[v].wait_recv()
        sh, sm, sl = split3(snap[v])
        a = jnp.dot(table3, sh, preferred_element_type=F32)
        b = jnp.dot(table3[: 2 * rows], sm, preferred_element_type=F32)
        c = jnp.dot(th, sl, preferred_element_type=F32)
        least = a[2 * rows :] + b[rows:] + c
        part[v] = a[:rows] + ((a[rows : 2 * rows] + b[:rows]) + least)
        for k, target in enumerate(targets):
            copy = pltpu.make_async_remote_copy(
                src_ref=part.at[v, pl.ds(pl.multiple_of(target * per, 8), per), :],
                dst_ref=got.at[group, v, :, my_cells],
                send_sem=psend_sem.at[k, v],
                recv_sem=precv_sem.at[k, v],
                device_id={"tm": target},
                device_id_type=MESH,
            )
            copy.start()
            sends.append((v, copy))
        got[group, v, :, my_cells] = part[v, pl.ds(pl.multiple_of(tm * per, 8), per), :]

    root = jnp.sqrt(vol_ref[...].reshape(1, cells))
    gram = jnp.zeros((3 * ROWS, 128), F32)
    outs = []
    for v in range(nvar):
        for w, copy in sends:
            if w == v:
                copy.wait_recv()
        pad = jnp.zeros((ROWS - per, cells), F32)
        first = jnp.concatenate([got[0, v], pad], axis=0)
        second = pltpu.roll(jnp.concatenate([got[1, v], pad], axis=0), 2 * fdev, 0)
        weighted = (first + second) * root
        wh, wm, wl = split3(weighted)
        lhs = jnp.concatenate([wh, wm, wl], axis=0)
        wcat[v] = lhs
        copy = pltpu.make_async_copy(wcat.at[v], wcat_hbm.at[v], out_sem.at[v])
        copy.start()
        outs.append(copy)
        rhs = jnp.concatenate([wh, wm, wl, jnp.zeros_like(wh)], axis=0)
        gram = gram + lax.dot_general(lhs, rhs, NT, preferred_element_type=F32)

    lane = lax.broadcasted_iota(jnp.int32, (ROWS, 128), 1)
    line = lax.broadcasted_iota(jnp.int32, (ROWS, 128), 0)
    gram = gram[:ROWS] + (gram[ROWS : 2 * ROWS] + gram[2 * ROWS :])
    gram = gram + (pltpu.roll(gram, 128 - ROWS, 1) + pltpu.roll(gram, 128 - 2 * ROWS, 1))
    gram = jnp.where(lane < ROWS, gram, 0.0)
    packed = gram[0:8]
    for q in range(1, ROWS // 8):
        packed = packed + pltpu.roll(gram[8 * q : 8 * q + 8], ROWS * q, 1)
    grams[cell] = packed

    gsends = []
    for step in range(1, cell_count):
        copy = pltpu.make_async_remote_copy(
            src_ref=grams.at[cell],
            dst_ref=grams.at[cell],
            send_sem=gsend_sem.at[step],
            recv_sem=grecv_sem.at[step],
            device_id={"cell": lax.rem(cell + step, cell_count)},
            device_id_type=MESH,
        )
        copy.start()
        gsends.append(copy)
    for copy in gsends:
        copy.wait_recv()
    total = grams[0]
    for q in range(1, cell_count):
        total = total + grams[q]

    total_ref[...] = total
    copy = pltpu.make_async_copy(total_ref, total_hbm, out_sem.at[nvar])
    copy.start()
    outs.append(copy)

    for copy in exchange:
        copy.wait_send()
    for _, copy in sends:
        copy.wait_send()
    for copy in gsends:
        copy.wait_send()
    for copy in outs:
        copy.wait()


def modes_kernel(
    sizes,
    wcat_hbm,
    total_hbm,
    modes_hbm,
    tri_hbm,
    wcat,
    total_ref,
    modes_ref,
    tri_ref,
    in_sem,
    out_sem,
):
    cell_count, tdev, nvar, cells, nf, nb = sizes
    fdev = nf // 4
    total_in = pltpu.make_async_copy(total_hbm, total_ref, in_sem.at[nvar])
    total_in.start()
    wcat_in = []
    for v in range(nvar):
        copy = pltpu.make_async_copy(wcat_hbm.at[v], wcat.at[v], in_sem.at[v])
        copy.start()
        wcat_in.append(copy)
    total_in.wait()
    lane = lax.broadcasted_iota(jnp.int32, (ROWS, 128), 1)
    line = lax.broadcasted_iota(jnp.int32, (ROWS, 128), 0)
    total = total_ref[...]
    pieces = [total] + [pltpu.roll(total, 128 - ROWS * q, 1) for q in range(1, ROWS // 8)]
    full = jnp.concatenate(pieces, axis=0)
    aug = jnp.where(lane < ROWS, full, jnp.where(lane - ROWS == line, 1.0, 0.0))
    columns = 2 * nb
    used = fdev * columns
    line_freq = (line // 2) % fdev
    order = jnp.where(line < used, (line % 2) * nb + line // (2 * fdev), -1)
    for j in range(columns - 1):
        base = (j % nb) * 2 * fdev + j // nb
        pivot = aug[base : base + 1, :]
        where = jnp.full((ROWS, 128), base, jnp.int32)
        for f in range(1, fdev):
            pivot = jnp.where(line_freq == f, aug[base + 2 * f : base + 2 * f + 1, :], pivot)
            where = jnp.where(line_freq == f, base + 2 * f, where)
        hit = lane == where
        column = jnp.sum(jnp.where(hit, aug, 0.0), axis=1, keepdims=True)
        diagonal = jnp.sum(jnp.where(hit, pivot, 0.0), axis=1, keepdims=True)
        factor = jnp.where(order > j, column / diagonal, 0.0)
        aug = aug - factor * pivot
    diagonal = jnp.sum(jnp.where(lane == line, aug, 0.0), axis=1, keepdims=True)
    diagonal = jnp.where(line < used, diagonal, 1.0)
    aug = aug * (1.0 / jnp.sqrt(diagonal))

    total_rows = nvar * cells * cell_count
    out_row = lax.broadcasted_iota(jnp.int32, (ROWS, ROWS), 0)
    in_row = lax.broadcasted_iota(jnp.int32, (ROWS, ROWS), 1)
    place = ((in_row % 2) * nb + in_row // (2 * fdev)) * fdev + (in_row // 2) % fdev
    permute = jnp.where((in_row < used) & (out_row == place), 1.0, 0.0)
    ordered = exact_dot(permute, aug)
    solve = ordered * jnp.sqrt(F32(total_rows))
    solve = jnp.where((lane >= ROWS) & (lane < 2 * ROWS), solve, 0.0)
    solve = solve + pltpu.roll(solve, 2 * ROWS, 1)
    solve = solve + pltpu.roll(solve, ROWS, 1)
    eh, em, el = [e.astype(F32) for e in split3(solve)]
    lhs = jnp.concatenate(
        [
            jnp.where(lane < 3 * ROWS, eh, em),
            jnp.where(lane < ROWS, em, jnp.where(lane < 2 * ROWS, el, 0.0)),
        ],
        axis=1,
    )[:, : 6 * ROWS].astype(BF16)
    copies = []
    for v in range(nvar):
        wcat_in[v].wait()
        held = wcat[v]
        rhs = jnp.concatenate([held, held[: 2 * ROWS], held[:ROWS]], axis=0)
        modes = jnp.dot(lhs, rhs, preferred_element_type=F32)
        for j in range(columns):
            modes_ref[v, j, :, :] = modes[j * fdev : (j + 1) * fdev, :]
        copy = pltpu.make_async_copy(modes_ref.at[v], modes_hbm.at[:, v], out_sem.at[v])
        copy.start()
        copies.append(copy)

    tri_scale = F32(1.0) / jnp.sqrt(F32(total_rows * NFFT))
    tri_out = lax.broadcasted_iota(jnp.int32, (16, 128), 0)
    tri_in = lax.broadcasted_iota(jnp.int32, (16, 128), 1)
    tri_row = lax.broadcasted_iota(jnp.int32, (ROWS, 16), 0)
    tri_lane = lax.broadcasted_iota(jnp.int32, (ROWS, 16), 1)
    tri = jnp.zeros((ROWS, 16), F32)
    for f in range(fdev):
        match = ((tri_in % 2) * nb + tri_in // (2 * fdev) == tri_out) & (
            (tri_in // 2) % fdev == f
        )
        picks = jnp.where(match & (tri_in < used), 1.0, 0.0)
        tri = jnp.where(tri_row % fdev == f, exact_dot(ordered, picks, NT), tri)
    tri = jnp.where(tri_row // fdev <= tri_lane, tri * tri_scale, 0.0)
    for j in range(columns):
        tri_ref[j] = tri[j * fdev : (j + 1) * fdev, :columns]
    copy = pltpu.make_async_copy(tri_ref, tri_hbm, out_sem.at[nvar])
    copy.start()
    copies.append(copy)
    for copy in copies:
        copy.wait()


def on_device(snapshots, volumes, freq_index, block_start):
    tdev, nvar, cells = snapshots.shape
    cell_count = lax.axis_size("cell")
    nf, nb = freq_index.shape[0], block_start.shape[0]
    fdev = nf // lax.axis_size("tm")
    columns = 2 * nb
    kept = nb - 1
    half = cells // 2
    per = kept * 2 * fdev
    sizes = (cell_count, tdev, nvar, cells, nf, nb)
    dma = pltpu.SemaphoreType.DMA
    hbm = pl.BlockSpec(memory_space=pltpu.HBM)
    wcat, total = pl.pallas_call(
        functools.partial(gather_kernel, sizes),
        out_shape=(
            jax.ShapeDtypeStruct((nvar, 3 * ROWS, cells), BF16),
            jax.ShapeDtypeStruct((8, 128), F32),
        ),
        in_specs=[hbm] * 4,
        out_specs=(hbm, hbm),
        scratch_shapes=[
            pltpu.VMEM((nvar, 3 * ROWS, cells), BF16),
            pltpu.VMEM((8, 128), F32),
            pltpu.VMEM((nvar, 2 * tdev, half), F32),
            pltpu.VMEM((nvar, nf * 2 * kept, half), F32),
            pltpu.VMEM((2, nvar, per, cells), F32),
            pltpu.VMEM((cell_count, 8, 128), F32),
            pltpu.VMEM((cells,), F32),
            pltpu.SMEM((nf,), jnp.int32),
            pltpu.SMEM((nb,), jnp.int32),
            dma((3,)),
            dma((nvar,)),
            dma((nvar,)),
            dma((nvar,)),
            dma((3, nvar)),
            dma((3, nvar)),
            dma((cell_count,)),
            dma((cell_count,)),
            dma((nvar + 1,)),
        ],
        compiler_params=pltpu.CompilerParams(
            collective_id=0, has_side_effects=True, vmem_limit_bytes=63 * 1024 * 1024
        ),
    )(jnp.transpose(snapshots, (1, 0, 2)), volumes, freq_index, block_start)
    modes, triangle = pl.pallas_call(
        functools.partial(modes_kernel, sizes),
        out_shape=(
            jax.ShapeDtypeStruct((columns, nvar, fdev, cells), F32),
            jax.ShapeDtypeStruct((columns, fdev, columns), F32),
        ),
        in_specs=[hbm, hbm],
        out_specs=(hbm, hbm),
        scratch_shapes=[
            pltpu.VMEM((nvar, 3 * ROWS, cells), BF16),
            pltpu.VMEM((8, 128), F32),
            pltpu.VMEM((nvar, columns, fdev, cells), F32),
            pltpu.VMEM((columns, fdev, columns), F32),
            dma((nvar + 1,)),
            dma((nvar + 1,)),
        ],
        compiler_params=pltpu.CompilerParams(vmem_limit_bytes=63 * 1024 * 1024),
    )(wcat, total)
    return jnp.transpose(modes, (2, 0, 1, 3)), jnp.transpose(triangle, (1, 0, 2))


def solution(mesh):
    placed = (P("tm", None, "cell"), P("cell"), P(), P())
    return jax.shard_map(
        on_device,
        mesh=mesh,
        in_specs=placed,
        out_specs=(P("tm", None, None, "cell"), P("tm", None, None)),
        check_vma=False,
    )
```

```python
import functools
import math

import jax
import jax.numpy as jnp
from jax import lax
from jax.experimental import pallas as pl
from jax.experimental.pallas import tpu as pltpu
from jax.sharding import PartitionSpec as P

NFFT = 128
MESH = pl.DeviceIdType.MESH
F32 = jnp.float32
BF16 = jnp.bfloat16
NT = (((1,), (1,)), ((), ()))
ROWS = 32


def split3(a):
    high = a.astype(BF16)
    rest = a - high.astype(F32)
    middle = rest.astype(BF16)
    low = (rest - middle.astype(F32)).astype(BF16)
    return high, middle, low


def half_sine_squared(step):
    near = ((step + NFFT // 2) & (NFFT - 1)) - NFFT // 2
    u = near.astype(F32) * (math.pi / NFFT)
    square = u * u
    total = jnp.full_like(u, 1.0 / math.factorial(13))
    for power in (11, 9, 7, 5, 3, 1):
        sign = 1.0 if power % 4 == 1 else -1.0
        total = total * square + sign / math.factorial(power)
    sine = u * total
    return sine * sine


def gather_kernel(
    sizes,
    x_ref,
    vol_hbm,
    freq_hbm,
    start_hbm,
    wcat_hbm,
    grams_hbm,
    wcat,
    packed_ref,
    snap,
    part,
    got,
    vol_ref,
    freq_ref,
    start_ref,
    small_sem,
    local_sem,
    xsend_sem,
    xrecv_sem,
    psend_sem,
    precv_sem,
    gsend_sem,
    grecv_sem,
    out_sem,
):
    cell_count, tdev, nvar, cells, nf, nb = sizes
    fdev = nf // 4
    kept = nb - 1
    half = cells // 2
    span = 2 * tdev
    per = kept * 2 * fdev
    rows = nf * 2 * kept
    cell = lax.axis_index("cell")
    tm = lax.axis_index("tm")
    group, core = tm // 2, lax.rem(tm, 2)
    partner = group * 2 + 1 - core
    targets = ((1 - group) * 2 + core, (1 - group) * 2 + 1 - core, partner)

    my_rows = pl.ds(pl.multiple_of(core * tdev, 8), tdev)
    my_cells = pl.ds(pl.multiple_of(core * half, 128), half)
    other_cells = pl.ds(pl.multiple_of((1 - core) * half, 128), half)

    barrier = pltpu.get_barrier_semaphore()
    for target in targets:
        pl.semaphore_signal(barrier, inc=1, device_id={"tm": target}, device_id_type=MESH)
    for step in range(1, cell_count):
        pl.semaphore_signal(
            barrier,
            inc=1,
            device_id={"cell": lax.rem(cell + step, cell_count)},
            device_id_type=MESH,
        )

    small = []
    for k, (src, dst) in enumerate(
        ((freq_hbm, freq_ref), (start_hbm, start_ref), (vol_hbm, vol_ref))
    ):
        copy = pltpu.make_async_copy(src, dst, small_sem.at[k])
        copy.start()
        small.append(copy)
    local = []
    for v in range(nvar):
        copy = pltpu.make_async_copy(
            x_ref.at[v, :, my_cells], snap.at[v, my_rows, :], local_sem.at[v]
        )
        copy.start()
        local.append(copy)

    pl.semaphore_wait(barrier, len(targets) + cell_count - 1)

    exchange = []
    for v in range(nvar):
        copy = pltpu.make_async_remote_copy(
            src_ref=x_ref.at[v, :, other_cells],
            dst_ref=snap.at[v, my_rows, :],
            send_sem=xsend_sem.at[v],
            recv_sem=xrecv_sem.at[v],
            device_id={"tm": partner},
            device_id_type=MESH,
        )
        exchange.append(copy)
    for v in range(min(2, nvar)):
        exchange[v].start()

    for copy in small:
        copy.wait()
    row = lax.broadcasted_iota(jnp.int32, (rows, span), 0)
    time = lax.broadcasted_iota(jnp.int32, (rows, span), 1) + group * span
    imag = (row // fdev) % 2
    row_block = (row // (2 * fdev)) % kept
    row_freq = (row // per) * fdev + row % fdev
    start = jnp.zeros((rows, span), jnp.int32)
    for b in range(kept):
        start = jnp.where(row_block == b, start_ref[group + b], start)
    freq = jnp.zeros((rows, span), jnp.int32)
    for f in range(nf):
        freq = jnp.where(row_freq == f, freq_ref[f], freq)
    tau = time - start
    valid = (tau >= 0) & (tau < NFFT)
    hann = jnp.where(valid, half_sine_squared(tau), 0.0)
    table = hann * (1.0 - 2.0 * half_sine_squared(freq * tau + imag * (NFFT // 4)))
    th, tmid, tl = split3(table)
    table3 = jnp.concatenate([th, tmid, tl], axis=0)

    sends = []
    for v in range(nvar):
        local[v].wait()
        exchange[v].wait_recv()
        if v + 2 < nvar:
            exchange[v + 2].start()
        sh, sm, sl = split3(snap[v])
        a = jnp.dot(table3, sh, preferred_element_type=F32)
        b = jnp.dot(table3[: 2 * rows], sm, preferred_element_type=F32)
        c = jnp.dot(th, sl, preferred_element_type=F32)
        least = a[2 * rows :] + b[rows:] + c
        part[v] = a[:rows] + ((a[rows : 2 * rows] + b[:rows]) + least)
        for k, target in enumerate(targets):
            copy = pltpu.make_async_remote_copy(
                src_ref=part.at[v, pl.ds(pl.multiple_of(target * per, 8), per), :],
                dst_ref=got.at[group, v, :, my_cells],
                send_sem=psend_sem.at[k, v],
                recv_sem=precv_sem.at[k, v],
                device_id={"tm": target},
                device_id_type=MESH,
            )
            copy.start()
            sends.append((v, copy))
        got[group, v, :, my_cells] = part[v, pl.ds(pl.multiple_of(tm * per, 8), per), :]

    root = jnp.sqrt(vol_ref[...].reshape(1, cells))
    gram = jnp.zeros((3 * ROWS, 128), F32)
    outs = []
    for v in range(nvar):
        for w, copy in sends:
            if w == v:
                copy.wait_recv()
        pad = jnp.zeros((ROWS - per, cells), F32)
        first = jnp.concatenate([got[0, v], pad], axis=0)
        second = pltpu.roll(jnp.concatenate([got[1, v], pad], axis=0), 2 * fdev, 0)
        weighted = (first + second) * root
        wh, wm, wl = split3(weighted)
        lhs = jnp.concatenate([wh, wm, wl], axis=0)
        wcat[v] = lhs
        copy = pltpu.make_async_copy(wcat.at[v], wcat_hbm.at[v], out_sem.at[v])
        copy.start()
        outs.append(copy)
        rhs = jnp.concatenate([wh, wm, wl, jnp.zeros_like(wh)], axis=0)
        gram = gram + lax.dot_general(lhs, rhs, NT, preferred_element_type=F32)

    gram = gram[:ROWS] + (gram[ROWS : 2 * ROWS] + gram[2 * ROWS :])
    lane = lax.broadcasted_iota(jnp.int32, (8, 128), 1)
    packed = jnp.zeros((8, 128), F32)
    for q in range(ROWS // 8):
        if 8 * q < 2 * nb * fdev:
            group_rows = gram[8 * q : 8 * q + 8]
            folded = sum(
                pltpu.roll(group_rows, ROWS * (q - s) % 128, 1) if q != s else group_rows
                for s in range(3)
            )
            packed = jnp.where(lane // ROWS == q, folded, packed)
    packed_ref[...] = packed

    own = pltpu.make_async_copy(packed_ref, grams_hbm.at[cell], out_sem.at[nvar])
    own.start()
    outs.append(own)
    gsends = []
    for step in range(1, cell_count):
        copy = pltpu.make_async_remote_copy(
            src_ref=packed_ref,
            dst_ref=grams_hbm.at[cell],
            send_sem=gsend_sem.at[step],
            recv_sem=grecv_sem.at[step],
            device_id={"cell": lax.rem(cell + step, cell_count)},
            device_id_type=MESH,
        )
        copy.start()
        gsends.append(copy)
    for copy in exchange:
        copy.wait_send()
    for _, copy in sends:
        copy.wait_send()
    for copy in outs:
        copy.wait()
    for copy in gsends:
        copy.wait_send()
        copy.wait_recv()


def modes_kernel(
    sizes,
    wcat_hbm,
    grams_hbm,
    modes_hbm,
    tri_hbm,
    wcat,
    grams,
    modes_ref,
    tri_ref,
    in_sem,
    out_sem,
):
    cell_count, tdev, nvar, cells, nf, nb = sizes
    fdev = nf // 4
    columns = 2 * nb
    used = fdev * columns
    height = -(-used // 8) * 8
    grams_in = pltpu.make_async_copy(grams_hbm, grams, in_sem.at[nvar])
    grams_in.start()
    wcat_in = []
    for v in range(nvar):
        copy = pltpu.make_async_copy(wcat_hbm.at[v], wcat.at[v], in_sem.at[v])
        copy.start()
        wcat_in.append(copy)

    lane = lax.broadcasted_iota(jnp.int32, (height, 128), 1)
    line = lax.broadcasted_iota(jnp.int32, (height, 128), 0)
    order = ((line // fdev) % 2) * nb + line // (2 * fdev)
    order = jnp.where(line < used, order, -1)
    bases = [(j % nb) * 2 * fdev + (j // nb) * fdev for j in range(columns)]
    tile_lane = lax.broadcasted_iota(jnp.int32, (8, 128), 1)
    tile_freq = lax.broadcasted_iota(jnp.int32, (8, 128), 0) % fdev

    grams_in.wait()
    total = grams[0]
    for q in range(1, cell_count):
        total = total + grams[q]

    def spread(base):
        pieces = []
        for q in range(height // 8):
            hit = tile_lane == ROWS * q + base + tile_freq
            piece = jnp.sum(jnp.where(hit, total, 0.0), axis=1, keepdims=True)
            pieces.append(jnp.broadcast_to(piece, (8, 128)))
        return jnp.concatenate(pieces, axis=0)

    def pivot_rows(a, base):
        pivot = jnp.broadcast_to(a[base : base + 1, :], (height, 128))
        for f in range(1, fdev):
            pivot = jnp.where(line % fdev == f, a[base + f : base + f + 1, :], pivot)
        return pivot

    gram = [spread(base) for base in bases]
    inverse = jnp.where(lane % ROWS == line, 1.0, 0.0)
    diagonal = jnp.ones((height, 128), F32)
    upper = jnp.zeros((height, 128), F32)
    for j in range(columns):
        diagonal = jnp.where(order == j, gram[j], diagonal)
        upper = jnp.where((lane == j) & (order <= j), gram[j], upper)
        if j + 1 < columns:
            factor = jnp.where(order > j, gram[j] / pivot_rows(gram[j], bases[j]), 0.0)
            for k in range(j + 1, columns):
                gram[k] = gram[k] - factor * pivot_rows(gram[k], bases[j])
            inverse = inverse - factor * pivot_rows(inverse, bases[j])
    scale = 1.0 / jnp.sqrt(diagonal)

    total_rows = nvar * cells * cell_count
    solve = inverse * (scale * jnp.sqrt(F32(total_rows)))
    solve = jnp.concatenate([solve, jnp.zeros((ROWS - height, 128), F32)], axis=0)
    eh, em, el = [e.astype(F32) for e in split3(solve)]
    wide = lax.broadcasted_iota(jnp.int32, (ROWS, 128), 1)
    lhs = jnp.concatenate(
        [jnp.where(wide < 3 * ROWS, eh, em), jnp.where(wide < ROWS, em, el)], axis=1
    )[:, : 6 * ROWS].astype(BF16)
    copies = []
    for v in range(nvar):
        wcat_in[v].wait()
        held = wcat[v]
        rhs = jnp.concatenate([held, held[: 2 * ROWS], held[:ROWS]], axis=0)
        modes = jnp.dot(lhs, rhs, preferred_element_type=F32)
        for j, base in enumerate(bases):
            modes_ref[v, j, :, :] = modes[base : base + fdev, :]
        copy = pltpu.make_async_copy(modes_ref.at[v], modes_hbm.at[:, v], out_sem.at[v])
        copy.start()
        copies.append(copy)
        if v == 0:
            tri = upper * (scale * (F32(1.0) / jnp.sqrt(F32(total_rows * NFFT))))
            for j, base in enumerate(bases):
                tri_ref[j] = tri[base : base + fdev, :columns]
            copy = pltpu.make_async_copy(tri_ref, tri_hbm, out_sem.at[nvar])
            copy.start()
            copies.append(copy)
    for copy in copies:
        copy.wait()


def on_device(snapshots, volumes, freq_index, block_start):
    tdev, nvar, cells = snapshots.shape
    cell_count = lax.axis_size("cell")
    nf, nb = freq_index.shape[0], block_start.shape[0]
    fdev = nf // lax.axis_size("tm")
    columns = 2 * nb
    kept = nb - 1
    half = cells // 2
    per = kept * 2 * fdev
    sizes = (cell_count, tdev, nvar, cells, nf, nb)
    dma = pltpu.SemaphoreType.DMA
    hbm = pl.BlockSpec(memory_space=pltpu.HBM)
    wcat, grams = pl.pallas_call(
        functools.partial(gather_kernel, sizes),
        out_shape=(
            jax.ShapeDtypeStruct((nvar, 3 * ROWS, cells), BF16),
            jax.ShapeDtypeStruct((cell_count, 8, 128), F32),
        ),
        in_specs=[hbm] * 4,
        out_specs=(hbm, hbm),
        scratch_shapes=[
            pltpu.VMEM((nvar, 3 * ROWS, cells), BF16),
            pltpu.VMEM((8, 128), F32),
            pltpu.VMEM((nvar, 2 * tdev, half), F32),
            pltpu.VMEM((nvar, nf * 2 * kept, half), F32),
            pltpu.VMEM((2, nvar, per, cells), F32),
            pltpu.VMEM((cells,), F32),
            pltpu.SMEM((nf,), jnp.int32),
            pltpu.SMEM((nb,), jnp.int32),
            dma((3,)),
            dma((nvar,)),
            dma((nvar,)),
            dma((nvar,)),
            dma((3, nvar)),
            dma((3, nvar)),
            dma((cell_count,)),
            dma((cell_count,)),
            dma((nvar + 1,)),
        ],
        compiler_params=pltpu.CompilerParams(
            collective_id=0, has_side_effects=True, vmem_limit_bytes=63 * 1024 * 1024
        ),
    )(jnp.transpose(snapshots, (1, 0, 2)), volumes, freq_index, block_start)
    modes, triangle = pl.pallas_call(
        functools.partial(modes_kernel, sizes),
        out_shape=(
            jax.ShapeDtypeStruct((columns, nvar, fdev, cells), F32),
            jax.ShapeDtypeStruct((columns, fdev, columns), F32),
        ),
        in_specs=[hbm, hbm],
        out_specs=(hbm, hbm),
        scratch_shapes=[
            pltpu.VMEM((nvar, 3 * ROWS, cells), BF16),
            pltpu.VMEM((cell_count, 8, 128), F32),
            pltpu.VMEM((nvar, columns, fdev, cells), F32),
            pltpu.VMEM((columns, fdev, columns), F32),
            dma((nvar + 1,)),
            dma((nvar + 1,)),
        ],
        compiler_params=pltpu.CompilerParams(vmem_limit_bytes=63 * 1024 * 1024),
    )(wcat, grams)
    return jnp.transpose(modes, (2, 0, 1, 3)), jnp.transpose(triangle, (1, 0, 2))


def solution(mesh):
    placed = (P("tm", None, "cell"), P("cell"), P(), P())
    return jax.shard_map(
        on_device,
        mesh=mesh,
        in_specs=placed,
        out_specs=(P("tm", None, None, "cell"), P("tm", None, None)),
        check_vma=False,
    )
```

```python
import functools
import math

import jax
import jax.numpy as jnp
from jax import lax
from jax.experimental import pallas as pl
from jax.experimental.pallas import tpu as pltpu
from jax.sharding import PartitionSpec as P

NFFT = 128
MESH = pl.DeviceIdType.MESH
F32 = jnp.float32
BF16 = jnp.bfloat16
NT = (((1,), (1,)), ((), ()))
ROWS = 32


def split3(a):
    high = a.astype(BF16)
    rest = a - high.astype(F32)
    middle = rest.astype(BF16)
    low = (rest - middle.astype(F32)).astype(BF16)
    return high, middle, low


def split2(a):
    high = a.astype(BF16)
    return high, (a - high.astype(F32)).astype(BF16)


def half_sine_squared(step):
    near = ((step + NFFT // 2) & (NFFT - 1)) - NFFT // 2
    u = near.astype(F32) * (math.pi / NFFT)
    square = u * u
    total = jnp.full_like(u, 1.0 / math.factorial(13))
    for power in (11, 9, 7, 5, 3, 1):
        sign = 1.0 if power % 4 == 1 else -1.0
        total = total * square + sign / math.factorial(power)
    sine = u * total
    return sine * sine


def gather_kernel(
    sizes,
    x_ref,
    vol_hbm,
    freq_hbm,
    start_hbm,
    wcat_hbm,
    grams_hbm,
    wcat,
    packed_ref,
    snap,
    part,
    near,
    chip,
    got,
    vol_ref,
    freq_ref,
    start_ref,
    small_sem,
    local_sem,
    xsend_sem,
    xrecv_sem,
    psend_sem,
    precv_sem,
    gsend_sem,
    grecv_sem,
    out_sem,
):
    cell_count, tdev, nvar, cells, nf, nb = sizes
    fdev = nf // 4
    kept = nb - 1
    per = kept * 2 * fdev
    rows = nf * 2 * kept
    cell = lax.axis_index("cell")
    tm = lax.axis_index("tm")
    group, core = tm // 2, lax.rem(tm, 2)
    partner = group * 2 + 1 - core
    across = (1 - group) * 2 + core

    barrier = pltpu.get_barrier_semaphore()
    for target in (partner, across):
        pl.semaphore_signal(barrier, inc=1, device_id={"tm": target}, device_id_type=MESH)
    for step in range(1, cell_count):
        pl.semaphore_signal(
            barrier,
            inc=1,
            device_id={"cell": lax.rem(cell + step, cell_count)},
            device_id_type=MESH,
        )

    small = []
    for k, (src, dst) in enumerate(
        ((freq_hbm, freq_ref), (start_hbm, start_ref), (vol_hbm, vol_ref))
    ):
        copy = pltpu.make_async_copy(src, dst, small_sem.at[k])
        copy.start()
        small.append(copy)
    local = []
    for v in range(nvar):
        copy = pltpu.make_async_copy(x_ref.at[v], snap.at[v], local_sem.at[v])
        copy.start()
        local.append(copy)

    for copy in small:
        copy.wait()
    row = lax.broadcasted_iota(jnp.int32, (rows, 2 * tdev), 0)
    time = lax.broadcasted_iota(jnp.int32, (rows, 2 * tdev), 1)
    time = jnp.where(time < tdev, time, time - tdev) + tm * tdev
    imag = (row // fdev) % 2
    row_block = (row // (2 * fdev)) % kept
    owner = ((row // per) % 2) * 2 + row // (2 * per)
    row_freq = owner * fdev + row % fdev
    start = jnp.zeros_like(row)
    for b in range(kept):
        start = jnp.where(row_block == b, start_ref[group + b], start)
    freq = jnp.zeros_like(row)
    for f in range(nf):
        freq = jnp.where(row_freq == f, freq_ref[f], freq)
    tau = time - start
    valid = (tau >= 0) & (tau < NFFT)
    hann = jnp.where(valid, half_sine_squared(tau), 0.0)
    table = hann * (1.0 - 2.0 * half_sine_squared(freq * tau + imag * (NFFT // 4)))
    th, tl = split2(table)
    table2 = jnp.concatenate([th, tl], axis=0)

    pair, sends = [], []

    def partial(v):
        local[v].wait()
        sh, sl = split2(snap[v])
        both = jnp.dot(
            table2, jnp.concatenate([sh, sl], axis=0), preferred_element_type=F32
        )
        part[v] = both[:rows] + both[rows:]
        if v == 0:
            pl.semaphore_wait(barrier, 2 + cell_count - 1)
        theirs = pl.ds(pl.multiple_of((1 - core) * 2 * per, 8), 2 * per)
        copy = pltpu.make_async_remote_copy(
            src_ref=part.at[v, theirs, :],
            dst_ref=near.at[v],
            send_sem=xsend_sem.at[v],
            recv_sem=xrecv_sem.at[v],
            device_id={"tm": partner},
            device_id_type=MESH,
        )
        copy.start()
        pair.append(copy)

    def forward(v):
        pair[v].wait_recv()
        mine = pl.ds(pl.multiple_of(core * 2 * per, 8), 2 * per)
        chip[v] = part[v, mine, :] + near[v]
        copy = pltpu.make_async_remote_copy(
            src_ref=chip.at[v, pl.ds(pl.multiple_of((1 - group) * per, 8), per), :],
            dst_ref=got.at[group, v],
            send_sem=psend_sem.at[v],
            recv_sem=precv_sem.at[v],
            device_id={"tm": across},
            device_id_type=MESH,
        )
        copy.start()
        sends.append(copy)
        got[group, v] = chip[v, pl.ds(pl.multiple_of(group * per, 8), per), :]

    lag = 2
    for v in range(nvar + lag):
        if v < nvar:
            partial(v)
        if v >= lag:
            forward(v - lag)

    root = jnp.sqrt(vol_ref[...].reshape(1, cells))
    gram = jnp.zeros((3 * ROWS, 128), F32)
    outs = []
    for v in range(nvar):
        sends[v].wait_recv()
        pad = jnp.zeros((ROWS - per, cells), F32)
        first = jnp.concatenate([got[0, v], pad], axis=0)
        second = pltpu.roll(jnp.concatenate([got[1, v], pad], axis=0), 2 * fdev, 0)
        weighted = (first + second) * root
        wh, wm, wl = split3(weighted)
        lhs = jnp.concatenate([wh, wm, wl], axis=0)
        wcat[v] = lhs
        copy = pltpu.make_async_copy(wcat.at[v], wcat_hbm.at[v], out_sem.at[v])
        copy.start()
        outs.append(copy)
        rhs = jnp.concatenate([wh, wm, wl, jnp.zeros_like(wh)], axis=0)
        gram = gram + lax.dot_general(lhs, rhs, NT, preferred_element_type=F32)

    gram = gram[:ROWS] + (gram[ROWS : 2 * ROWS] + gram[2 * ROWS :])
    lane = lax.broadcasted_iota(jnp.int32, (8, 128), 1)
    packed = jnp.zeros((8, 128), F32)
    for q in range(ROWS // 8):
        if 8 * q < 2 * nb * fdev:
            group_rows = gram[8 * q : 8 * q + 8]
            folded = sum(
                pltpu.roll(group_rows, ROWS * (q - s) % 128, 1) if q != s else group_rows
                for s in range(3)
            )
            packed = jnp.where(lane // ROWS == q, folded, packed)
    packed_ref[...] = packed

    own = pltpu.make_async_copy(packed_ref, grams_hbm.at[cell], out_sem.at[nvar])
    own.start()
    outs.append(own)
    gsends = []
    for step in range(1, cell_count):
        copy = pltpu.make_async_remote_copy(
            src_ref=packed_ref,
            dst_ref=grams_hbm.at[cell],
            send_sem=gsend_sem.at[step],
            recv_sem=grecv_sem.at[step],
            device_id={"cell": lax.rem(cell + step, cell_count)},
            device_id_type=MESH,
        )
        copy.start()
        gsends.append(copy)
    for copy in pair + sends:
        copy.wait_send()
    for copy in outs:
        copy.wait()
    for copy in gsends:
        copy.wait_send()
        copy.wait_recv()


def modes_kernel(
    sizes,
    wcat_hbm,
    grams_hbm,
    modes_hbm,
    tri_hbm,
    wcat,
    grams,
    modes_ref,
    tri_ref,
    in_sem,
    out_sem,
):
    cell_count, tdev, nvar, cells, nf, nb = sizes
    fdev = nf // 4
    columns = 2 * nb
    used = fdev * columns
    height = -(-used // 8) * 8
    grams_in = pltpu.make_async_copy(grams_hbm, grams, in_sem.at[nvar])
    grams_in.start()
    wcat_in = []
    for v in range(nvar):
        copy = pltpu.make_async_copy(wcat_hbm.at[v], wcat.at[v], in_sem.at[v])
        copy.start()
        wcat_in.append(copy)

    lane = lax.broadcasted_iota(jnp.int32, (height, 128), 1)
    line = lax.broadcasted_iota(jnp.int32, (height, 128), 0)
    order = ((line // fdev) % 2) * nb + line // (2 * fdev)
    order = jnp.where(line < used, order, -1)
    bases = [(j % nb) * 2 * fdev + (j // nb) * fdev for j in range(columns)]
    tile_lane = lax.broadcasted_iota(jnp.int32, (8, 128), 1)
    tile_freq = lax.broadcasted_iota(jnp.int32, (8, 128), 0) % fdev

    grams_in.wait()
    total = grams[0]
    for q in range(1, cell_count):
        total = total + grams[q]

    def spread(base):
        pieces = []
        for q in range(height // 8):
            hit = tile_lane == ROWS * q + base + tile_freq
            piece = jnp.sum(jnp.where(hit, total, 0.0), axis=1, keepdims=True)
            pieces.append(jnp.broadcast_to(piece, (8, 128)))
        return jnp.concatenate(pieces, axis=0)

    def pivot_rows(a, base):
        pivot = jnp.broadcast_to(a[base : base + 1, :], (height, 128))
        for f in range(1, fdev):
            pivot = jnp.where(line % fdev == f, a[base + f : base + f + 1, :], pivot)
        return pivot

    gram = [spread(base) for base in bases]
    inverse = jnp.where(lane % ROWS == line, 1.0, 0.0)
    diagonal = jnp.ones((height, 128), F32)
    upper = jnp.zeros((height, 128), F32)
    for j in range(columns):
        diagonal = jnp.where(order == j, gram[j], diagonal)
        upper = jnp.where((lane == j) & (order <= j), gram[j], upper)
        if j + 1 < columns:
            factor = jnp.where(order > j, gram[j] / pivot_rows(gram[j], bases[j]), 0.0)
            for k in range(j + 1, columns):
                gram[k] = gram[k] - factor * pivot_rows(gram[k], bases[j])
            inverse = inverse - factor * pivot_rows(inverse, bases[j])
    scale = 1.0 / jnp.sqrt(diagonal)

    total_rows = nvar * cells * cell_count
    solve = inverse * (scale * jnp.sqrt(F32(total_rows)))
    solve = jnp.concatenate([solve, jnp.zeros((ROWS - height, 128), F32)], axis=0)
    eh, em, el = [e.astype(F32) for e in split3(solve)]
    wide = lax.broadcasted_iota(jnp.int32, (ROWS, 128), 1)
    lhs = jnp.concatenate(
        [jnp.where(wide < 3 * ROWS, eh, em), jnp.where(wide < ROWS, em, el)], axis=1
    )[:, : 6 * ROWS].astype(BF16)
    copies = []
    for v in range(nvar):
        wcat_in[v].wait()
        held = wcat[v]
        rhs = jnp.concatenate([held, held[: 2 * ROWS], held[:ROWS]], axis=0)
        modes = jnp.dot(lhs, rhs, preferred_element_type=F32)
        for j, base in enumerate(bases):
            modes_ref[v, j, :, :] = modes[base : base + fdev, :]
        copy = pltpu.make_async_copy(modes_ref.at[v], modes_hbm.at[:, v], out_sem.at[v])
        copy.start()
        copies.append(copy)
        if v == 0:
            tri = upper * (scale * (F32(1.0) / jnp.sqrt(F32(total_rows * NFFT))))
            for j, base in enumerate(bases):
                tri_ref[j] = tri[base : base + fdev, :columns]
            copy = pltpu.make_async_copy(tri_ref, tri_hbm, out_sem.at[nvar])
            copy.start()
            copies.append(copy)
    for copy in copies:
        copy.wait()


def on_device(snapshots, volumes, freq_index, block_start):
    tdev, nvar, cells = snapshots.shape
    cell_count = lax.axis_size("cell")
    nf, nb = freq_index.shape[0], block_start.shape[0]
    fdev = nf // lax.axis_size("tm")
    columns = 2 * nb
    kept = nb - 1
    per = kept * 2 * fdev
    sizes = (cell_count, tdev, nvar, cells, nf, nb)
    dma = pltpu.SemaphoreType.DMA
    hbm = pl.BlockSpec(memory_space=pltpu.HBM)
    wcat, grams = pl.pallas_call(
        functools.partial(gather_kernel, sizes),
        out_shape=(
            jax.ShapeDtypeStruct((nvar, 3 * ROWS, cells), BF16),
            jax.ShapeDtypeStruct((cell_count, 8, 128), F32),
        ),
        in_specs=[hbm] * 4,
        out_specs=(hbm, hbm),
        scratch_shapes=[
            pltpu.VMEM((nvar, 3 * ROWS, cells), BF16),
            pltpu.VMEM((8, 128), F32),
            pltpu.VMEM((nvar, tdev, cells), F32),
            pltpu.VMEM((nvar, nf * 2 * kept, cells), F32),
            pltpu.VMEM((nvar, 2 * per, cells), F32),
            pltpu.VMEM((nvar, 2 * per, cells), F32),
            pltpu.VMEM((2, nvar, per, cells), F32),
            pltpu.VMEM((cells,), F32),
            pltpu.SMEM((nf,), jnp.int32),
            pltpu.SMEM((nb,), jnp.int32),
            dma((3,)),
            dma((nvar,)),
            dma((nvar,)),
            dma((nvar,)),
            dma((nvar,)),
            dma((nvar,)),
            dma((cell_count,)),
            dma((cell_count,)),
            dma((nvar + 1,)),
        ],
        compiler_params=pltpu.CompilerParams(
            collective_id=0, has_side_effects=True, vmem_limit_bytes=63 * 1024 * 1024
        ),
    )(jnp.transpose(snapshots, (1, 0, 2)), volumes, freq_index, block_start)
    modes, triangle = pl.pallas_call(
        functools.partial(modes_kernel, sizes),
        out_shape=(
            jax.ShapeDtypeStruct((columns, nvar, fdev, cells), F32),
            jax.ShapeDtypeStruct((columns, fdev, columns), F32),
        ),
        in_specs=[hbm, hbm],
        out_specs=(hbm, hbm),
        scratch_shapes=[
            pltpu.VMEM((nvar, 3 * ROWS, cells), BF16),
            pltpu.VMEM((cell_count, 8, 128), F32),
            pltpu.VMEM((nvar, columns, fdev, cells), F32),
            pltpu.VMEM((columns, fdev, columns), F32),
            dma((nvar + 1,)),
            dma((nvar + 1,)),
        ],
        compiler_params=pltpu.CompilerParams(vmem_limit_bytes=63 * 1024 * 1024),
    )(wcat, grams)
    return jnp.transpose(modes, (2, 0, 1, 3)), jnp.transpose(triangle, (1, 0, 2))


def solution(mesh):
    placed = (P("tm", None, "cell"), P("cell"), P(), P())
    return jax.shard_map(
        on_device,
        mesh=mesh,
        in_specs=placed,
        out_specs=(P("tm", None, None, "cell"), P("tm", None, None)),
        check_vma=False,
    )
```
